256 devices in a mesh: ctx: 32 (over z, y), head: 8 (over x, core).
Axes of the slice: x: 4, y: 4, z: 8, core: 2. Of those that a mesh axis runs over, the one named last changes fastest.
Arguments:
- queries: bfloat16 [8192, 8192], P('ctx', 'head'), may hold values from -6 to 6
- key_rows: bfloat16 [8192, 1024], P('ctx', 'head'), may hold values from -6 to 6
- value_rows: bfloat16 [8192, 1024], P('ctx', 'head'), may hold values from -6 to 6
- out_grads: bfloat16 [8192, 8192], P(('ctx', 'head')), may hold values from -6 to 6
- doc_ids: int32 [8192], replicated, may hold values from 0 to 7, never falling along the last dimension, each value on 1 to 4096 neighbouring positions
- owner_plan: int32 [32, 32], replicated, may hold values from 0 to 31, each once within a row
Outputs:
- attention: bfloat16 [8192, 8192], P(('ctx', 'head'))
- query_grads: bfloat16 [8192, 8192], P('ctx', 'head')
- key_grads: bfloat16 [8192, 1024], P('ctx', 'head')
- value_grads: bfloat16 [8192, 1024], P('ctx', 'head')
The draws below stay inside these ranges and needn't reach their ends.
Inputs may be any that keep to these rules, and one draw needn't show every extreme that they name: `owner_plan`: row d lists the owners of the 32 pieces of index d of ctx; each owner once in every row.
All inputs are finite; a program needn't handle non-finite values.
Results may differ from the reference program's by a relative error of at most 0.027.
Values may be sent and summed in bfloat16 or wider, within the bound.
No kernel may reach another device: no remote copies, remote signals or barrier semaphores. Data moves between devices by JAX's collectives and lax.ppermute only.
A program may use at most 64 MiB of HBM per device.

```python
import math
import jax
import jax.numpy as jnp
import numpy as np
from jax import lax

HD = 128
QH = 64
KVH = 8
TOK_DEV = 256
KTILE = 512
TOKENS = 8192
DOCLEN = 4096
DOCS = 8
N_CTX = 32


def draw_queries(key, part):
    own_key = jax.random.fold_in(key, 3)
    base = jnp.clip(jax.random.normal(own_key, (TOKENS, QH, HD), jnp.float32), -6.0, 6.0)
    return base.reshape(TOKENS, QH * HD).astype(jnp.bfloat16)


def draw_key_rows(key, part):
    own_key = jax.random.fold_in(key, 5)
    base = jnp.clip(jax.random.normal(own_key, (TOKENS, KVH, HD), jnp.float32), -6.0, 6.0)
    return base.reshape(TOKENS, KVH * HD).astype(jnp.bfloat16)


def steps_of(rng, extent, split, low, high):
    def one(position, parts):
        steps = jax.random.uniform(jax.random.fold_in(jax.random.fold_in(rng, 6), position), (parts,), jnp.float32, low / len(split), high / len(split))
        return jnp.repeat(jnp.exp(steps), extent[position] // parts).reshape((-1,) + (1,) * (len(extent) - position - 1))

    loudness = one(*split[0])
    for cut in split[1:]:
        loudness = loudness * one(*cut)
    return loudness


def profile(count, total, bound, lean):
    portions = [(1 << 20) // math.isqrt(standing ** lean) + 1 for standing in range(2, count + 1)]
    surplus, holding = total - bound - (count - 1), [1] * (count - 1)
    while surplus > 0:
        free = [i for i in range(count - 1) if holding[i] < bound]
        pool, budget = sum([portions[i] for i in free]), surplus
        for i in free:
            more = min(bound - holding[i], max(1, budget * portions[i] // pool), surplus)
            holding[i] = holding[i] + more
            surplus = surplus - more
    return np.array([bound] + holding)


def uneven(stream_key, amount, total, reach, lean):
    if amount == 2:
        one = jax.random.randint(stream_key, (), max(1, total - reach), min(reach, total - 1) + 1)
        return jnp.stack([one, total - one])
    tallies = jnp.asarray(profile(amount, total, reach, lean), jnp.int32)
    pairs = (amount - 1) // 2
    donor, receiver = tallies[1:1 + 2 * pairs:2], tallies[2:2 + 2 * pairs:2]
    room = jnp.minimum(donor - 1, reach - receiver)
    moved = jax.random.randint(jax.random.fold_in(stream_key, 1), (pairs,), 0, 1 << 20) % (room + 1)
    tallies = tallies.at[1:1 + 2 * pairs:2].set(donor - moved).at[2:2 + 2 * pairs:2].set(receiver + moved)
    return tallies[jax.random.permutation(jax.random.fold_in(stream_key, 2), amount)]


def normal_values(rng, dims, spread, most, split=(), kind=jnp.bfloat16):
    factor_of = steps_of(rng, dims, split, -0.22, 0.18) if split else 1.0
    entries = jax.random.normal(rng, dims, jnp.float32) * spread * factor_of
    return jnp.minimum(jnp.maximum(entries, -most), most).astype(kind)


def setup_inputs(seed: int = 0) -> dict:
    keys = jax.random.split(jax.random.key(seed), 7)
    queries = draw_queries(jax.random.fold_in(keys[6], 71), 0)
    key_rows = draw_key_rows(jax.random.fold_in(keys[6], 71), 0)
    value_rows = normal_values(keys[2], (TOKENS, KVH * HD), 1.0, 6.0, ((0, 32), (1, 8)))
    out_grads = normal_values(keys[3], (TOKENS, QH * HD), 1.0, 6.0, ((0, 256),))
    doc_ids = jnp.searchsorted(jnp.cumsum(uneven(keys[4], DOCS, TOKENS, DOCLEN, 2)), jnp.arange(TOKENS), side="right").astype(jnp.int32)
    owner_plan = jax.vmap(lambda own: jax.random.permutation(own, N_CTX))(jax.random.split(keys[5], N_CTX)).reshape((N_CTX, N_CTX)).astype(jnp.int32)
    return {"queries": queries, "key_rows": key_rows, "value_rows": value_rows, "out_grads": out_grads, "doc_ids": doc_ids, "owner_plan": owner_plan}


MASKED = -1.0e30


def doc_starts(doc_ids):
    count = doc_ids.shape[0]
    places = jnp.arange(count, dtype=jnp.int32)
    fresh = jnp.concatenate([jnp.ones((1,), dtype=bool), doc_ids[1:] != doc_ids[:-1]])
    return lax.cummax(jnp.where(fresh, places, 0).astype(jnp.int32), axis=0)


def reference(queries, key_rows, value_rows, out_grads, doc_ids, owner_plan):
    per_kv = QH // KVH
    scale = HD ** -0.5
    qrow = TOK_DEV // N_CTX
    inverse = jnp.argsort(owner_plan, axis=1).astype(jnp.int32)
    devices = jnp.arange(N_CTX, dtype=jnp.int32)
    inner = jnp.arange(qrow, dtype=jnp.int32)
    back_map = (owner_plan[:, :, None] * TOK_DEV + devices[:, None, None] * qrow + inner[None, None, :]).reshape(-1)
    order_map = (devices[None, :, None] * TOK_DEV + inverse.T[:, :, None] * qrow + inner[None, None, :]).reshape(-1)
    grads_home = out_grads[back_map]
    starts = doc_starts(doc_ids)
    query_four = queries.reshape(TOKENS, KVH, per_kv, HD)
    grad_four = grads_home.reshape(TOKENS, KVH, per_kv, HD)
    key_three = key_rows.reshape(TOKENS, KVH, HD)
    value_three = value_rows.reshape(TOKENS, KVH, HD)
    block_count = TOKENS // KTILE

    def block_step(block_index, state):
        attn_all, dq_all, part_k, part_v = state
        row_start = block_index * KTILE
        row_places = row_start + jnp.arange(KTILE, dtype=jnp.int32)
        query_block = lax.dynamic_slice_in_dim(query_four, row_start, KTILE, 0).astype(jnp.float32)
        grad_block = lax.dynamic_slice_in_dim(grad_four, row_start, KTILE, 0).astype(jnp.float32)
        row_docs = lax.dynamic_slice_in_dim(doc_ids, row_start, KTILE, 0)
        first_tile = jnp.min(lax.dynamic_slice_in_dim(starts, row_start, KTILE, 0)) // KTILE
        end_tile = block_index + 1

        def tile_at(tile_index):
            key_start = tile_index * KTILE
            key_tile = lax.dynamic_slice_in_dim(key_three, key_start, KTILE, 0).astype(jnp.float32)
            value_tile = lax.dynamic_slice_in_dim(value_three, key_start, KTILE, 0).astype(jnp.float32)
            key_docs = lax.dynamic_slice_in_dim(doc_ids, key_start, KTILE, 0)
            key_places = key_start + jnp.arange(KTILE, dtype=jnp.int32)
            visible = (key_docs[None, :] == row_docs[:, None]) & (key_places[None, :] <= row_places[:, None])
            visible = visible[:, None, None, :]
            logits = jnp.einsum("rghd,kgd->rghk", query_block, key_tile) * scale
            return logits, visible, key_tile, value_tile

        def first_pass(tile_index, carry):
            row_peak, row_total = carry
            logits, visible, unused_k, unused_v = tile_at(tile_index)
            logits = jnp.where(visible, logits, MASKED)
            new_peak = jnp.maximum(row_peak, jnp.max(logits, axis=-1))
            weights = jnp.where(visible, jnp.exp(logits - new_peak[..., None]), 0.0)
            row_total = row_total * jnp.exp(row_peak - new_peak) + jnp.sum(weights, axis=-1)
            return new_peak, row_total

        start_peak = jnp.full((KTILE, KVH, per_kv), MASKED, jnp.float32)
        start_total = jnp.zeros((KTILE, KVH, per_kv), jnp.float32)
        row_peak, row_total = lax.fori_loop(first_tile, end_tile, first_pass, (start_peak, start_total))
        lse = row_peak + jnp.log(row_total)

        def second_pass(tile_index, summed):
            logits, visible, unused_k, value_tile = tile_at(tile_index)
            probs = jnp.where(visible, jnp.exp(logits - lse[..., None]), 0.0).astype(jnp.bfloat16)
            probs = lax.optimization_barrier(probs).astype(jnp.float32)
            return summed + jnp.einsum("rghk,kgd->rghd", probs, value_tile)

        summed = lax.fori_loop(first_tile, end_tile, second_pass, jnp.zeros((KTILE, KVH, per_kv, HD), jnp.float32))
        attn_block = summed.astype(jnp.bfloat16)
        delta = jnp.sum(grad_block * attn_block.astype(jnp.float32), axis=-1)

        def third_pass(tile_index, carry):
            grad_q, part_k, part_v = carry
            logits, visible, key_tile, value_tile = tile_at(tile_index)
            probs = jnp.where(visible, jnp.exp(logits - lse[..., None]), 0.0)
            prob_low = lax.optimization_barrier(probs.astype(jnp.bfloat16)).astype(jnp.float32)
            dprob = jnp.einsum("rghd,kgd->rghk", grad_block, value_tile)
            dlogit = (probs * (dprob - delta[..., None])).astype(jnp.bfloat16)
            dlogit = lax.optimization_barrier(dlogit).astype(jnp.float32)
            grad_q = grad_q + jnp.einsum("rghk,kgd->rghd", dlogit, key_tile)
            key_start = tile_index * KTILE
            key_term = jnp.einsum("rghk,rghd->kgd", dlogit, query_block)
            value_term = jnp.einsum("rghk,rghd->kgd", prob_low, grad_block)
            old_k = lax.dynamic_slice_in_dim(part_k, key_start, KTILE, 0)
            old_v = lax.dynamic_slice_in_dim(part_v, key_start, KTILE, 0)
            part_k = lax.dynamic_update_slice_in_dim(part_k, old_k + key_term, key_start, 0)
            part_v = lax.dynamic_update_slice_in_dim(part_v, old_v + value_term, key_start, 0)
            return grad_q, part_k, part_v

        start_grad = jnp.zeros((KTILE, KVH, per_kv, HD), jnp.float32)
        grad_q, part_k, part_v = lax.fori_loop(first_tile, end_tile, third_pass, (start_grad, part_k, part_v))
        attn_all = lax.dynamic_update_slice_in_dim(attn_all, attn_block, row_start, 0)
        dq_all = lax.dynamic_update_slice_in_dim(dq_all, (grad_q * scale).astype(jnp.bfloat16), row_start, 0)
        return attn_all, dq_all, part_k, part_v

    start_state = (
        jnp.zeros((TOKENS, KVH, per_kv, HD), jnp.bfloat16),
        jnp.zeros((TOKENS, KVH, per_kv, HD), jnp.bfloat16),
        jnp.zeros((TOKENS, KVH, HD), jnp.float32),
        jnp.zeros((TOKENS, KVH, HD), jnp.float32),
    )
    attn_all, dq_all, part_k, part_v = lax.fori_loop(0, block_count, block_step, start_state)
    attention = attn_all.reshape(TOKENS, QH * HD)[order_map]
    query_grads = dq_all.reshape(TOKENS, QH * HD)
    key_grads = (part_k * scale).astype(jnp.bfloat16).reshape(TOKENS, KVH * HD)
    value_grads = part_v.astype(jnp.bfloat16).reshape(TOKENS, KVH * HD)
    return attention, query_grads, key_grads, value_grads
```

```python
import jax
import jax.numpy as jnp
from jax import lax
from jax.experimental import pallas as pl
from jax.experimental.pallas import tpu as pltpu
from jax.sharding import PartitionSpec as P

HD = 128
NZ = 8
NY = 4
TOK = 256
PIECE = 8
KB = 512
DOCLEN = 4096
DOCS = 8
GROUPS = 8
MASKED = -1e30
LOG2E = 1.4426950408889634
f32 = jnp.float32
bf16 = jnp.bfloat16


def attend_kernel(
    lo_ref, hi_ref, at_ref, place_ref, start_ref, q_ref, g_ref, *refs
):
    k_refs, v_refs = refs[:NZ], refs[NZ : NZ + 5]
    o_ref, dq_ref = refs[NZ + 5 : NZ + 7]
    dk_refs = refs[NZ + 7 : 2 * NZ + 7]
    dv_refs = refs[2 * NZ + 7 : 2 * NZ + 15]
    kt, vt, kn, vn, dk_acc, dv_acc, s_ref, e_ref = refs[2 * NZ + 15 :]
    rows, width = q_ref.shape
    heads = width // HD
    span = rows // GROUPS
    lanes = span * heads
    scale = HD**-0.5
    zc = NY * TOK
    my_z, my_y = at_ref[0], at_ref[1]

    for s in range(NZ):
        z = lax.rem(my_z + NZ - s, NZ)
        at = pl.ds(pl.multiple_of(z * zc, zc), zc)
        kn[at, :] = k_refs[s][...]
        for b in range(zc // KB):
            kt[z * (zc // KB) + b] = k_refs[s][b * KB : (b + 1) * KB, :].T

    def place_v(ref, shift, z_from, z_count):
        y = lax.rem(my_y + NY - shift, NY)
        for z in range(z_count):
            at = pl.ds(pl.multiple_of((z_from + z) * zc + y * TOK, TOK), TOK)
            vn[at, :] = ref[z * TOK : (z + 1) * TOK, :]

    place_v(v_refs[0], 0, 0, NZ)
    place_v(v_refs[1], 1, 0, NZ)
    place_v(v_refs[2], 3, 0, NZ)
    place_v(v_refs[3], 2, 0, NZ // 2)
    place_v(v_refs[4], 2, NZ // 2, NZ // 2)

    def prepare(b, carry):
        at = pl.ds(pl.multiple_of(b * KB, KB), KB)
        vt[b] = vn[at, :].T
        dk_acc[at, :] = jnp.zeros((KB, HD), f32)
        dv_acc[at, :] = jnp.zeros((KB, HD), f32)
        return carry

    lax.fori_loop(0, NZ * zc // KB, prepare, 0)

    def gather_heads(ref, at):
        x = ref[at, :]
        return jnp.concatenate([x[:, h * HD : (h + 1) * HD] for h in range(heads)], axis=0)

    def scatter_heads(ref, at, x):
        for h in range(heads):
            ref[at, h * HD : (h + 1) * HD] = x[h * span : (h + 1) * span]

    def group(gi, carry):
        at = pl.ds(pl.multiple_of(gi * span, span), span)
        lo, hi = lo_ref[gi], hi_ref[gi]
        place, start = place_ref[gi], start_ref[gi]
        qt = gather_heads(q_ref, at).astype(f32).T
        gt = gather_heads(g_ref, at).astype(f32).T
        qtb, gtb = qt.astype(bf16), gt.astype(bf16)

        def score(kb, peak):
            keys = pl.ds(pl.multiple_of(kb * KB, KB), KB)
            s = jnp.dot(kn[keys, :], qtb, preferred_element_type=f32)
            u = kb * KB + lax.broadcasted_iota(jnp.int32, (KB, lanes), 0)
            s = jnp.where((u >= start) & (u <= place), s, MASKED)
            s_ref[kb - lo] = s
            return jnp.maximum(peak, jnp.max(s.reshape(KB // 8, 8, lanes), axis=0))

        peak = lax.fori_loop(lo, hi, score, jnp.full((8, lanes), MASKED, f32))
        peak = jnp.max(peak, axis=0, keepdims=True) * (scale * LOG2E)

        def weigh(kb, carry):
            ot, total = carry
            e = jnp.exp2(s_ref[kb - lo] * (scale * LOG2E) - peak)
            eb = e.astype(bf16)
            e_ref[kb - lo] = eb
            total = total + jnp.sum(e.reshape(KB // 8, 8, lanes), axis=0)
            ot = ot + jnp.dot(vt[kb], eb, preferred_element_type=f32)
            return ot, total

        ot, total = lax.fori_loop(
            lo, hi, weigh, (jnp.zeros((HD, lanes), f32), jnp.zeros((8, lanes), f32))
        )
        inverse = 1.0 / jnp.sum(total, axis=0, keepdims=True)
        otb = (ot * inverse).astype(bf16).astype(f32)
        scatter_heads(o_ref, at, otb.T.astype(bf16))
        delta = jnp.sum(otb * gt, axis=0, keepdims=True)
        qs = (qt * inverse).T.astype(bf16)
        gs = (gt * inverse).T.astype(bf16)

        def back(kb, dqt):
            keys = pl.ds(pl.multiple_of(kb * KB, KB), KB)
            dp = jnp.dot(vn[keys, :], gtb, preferred_element_type=f32)
            eb = e_ref[kb - lo]
            ds = (eb.astype(f32) * (dp - delta)).astype(bf16)
            dk_acc[keys, :] += jnp.dot(ds, qs, preferred_element_type=f32)
            dv_acc[keys, :] += jnp.dot(eb, gs, preferred_element_type=f32)
            return dqt + jnp.dot(kt[kb], ds, preferred_element_type=f32)

        dqt = lax.fori_loop(lo, hi, back, jnp.zeros((HD, lanes), f32))
        scatter_heads(dq_ref, at, (dqt * (inverse * scale)).T.astype(bf16))
        return carry

    lax.fori_loop(0, GROUPS, group, 0)

    for r in range(NZ):
        z = lax.rem(my_z + r, NZ)
        at = pl.ds(pl.multiple_of(z * zc, zc), zc)
        dk_refs[r][...] = (dk_acc[at, :] * scale).astype(bf16)
    for r in range(NY):
        y = lax.rem(my_y + r, NY)
        for z in range(NZ):
            half, inside = divmod(z, NZ // 2)
            at = pl.ds(pl.multiple_of(z * zc + y * TOK, TOK), TOK)
            dv_refs[2 * r + half][inside * TOK : (inside + 1) * TOK, :] = dv_acc[at, :].astype(bf16)


def attend(lo, hi, at, place, start, q, g, ks, vs):
    rows, width = q.shape
    total = NZ * NY * TOK
    lanes = rows // GROUPS * (width // HD)
    most = (DOCLEN + rows // GROUPS // PIECE * TOK) // KB
    vm = pl.BlockSpec(memory_space=pltpu.VMEM)
    sm = pl.BlockSpec(memory_space=pltpu.SMEM)
    outs = (
        [jax.ShapeDtypeStruct((rows, width), bf16)] * 2
        + [jax.ShapeDtypeStruct((NY * TOK, HD), bf16)] * NZ
        + [jax.ShapeDtypeStruct((NZ // 2 * TOK, HD), bf16)] * (2 * NY)
    )
    out = pl.pallas_call(
        attend_kernel,
        in_specs=[sm] * 3 + [vm] * (4 + len(ks) + len(vs)),
        out_specs=[vm] * len(outs),
        out_shape=outs,
        scratch_shapes=[
            pltpu.VMEM((total // KB, HD, KB), bf16),
            pltpu.VMEM((total // KB, HD, KB), bf16),
            pltpu.VMEM((total, HD), bf16),
            pltpu.VMEM((total, HD), bf16),
            pltpu.VMEM((total, HD), f32),
            pltpu.VMEM((total, HD), f32),
            pltpu.VMEM((most, KB, lanes), f32),
            pltpu.VMEM((most, KB, lanes), bf16),
        ],
        compiler_params=pltpu.CompilerParams(vmem_limit_bytes=56 * 1024 * 1024),
        cost_estimate=pl.CostEstimate(
            flops=12 * 10**9, bytes_accessed=12 * 10**6, transcendentals=4 * 10**6
        ),
        name="attend",
    )(lo, hi, at, place, start, q, g, *ks, *vs)
    return out[0], out[1], out[2 : 2 + NZ], out[2 + NZ :]


def shift(x, dz, dy):
    pairs = [
        (z * NY + y, (z + dz) % NZ * NY + (y + dy) % NY) for z in range(NZ) for y in range(NY)
    ]
    return lax.ppermute(x, "ctx", pairs)


Z_GROUPS = [[z * NY + y for z in range(NZ)] for y in range(NY)]
Y_GROUPS = [[z * NY + y for y in range(NY)] for z in range(NZ)]


def swap(x, groups):
    return lax.all_to_all(x, "ctx", 0, 0, axis_index_groups=groups, tiled=True)


def spread(x, groups):
    n = len(groups[0])
    return swap(jnp.broadcast_to(x[None], (n,) + x.shape), groups).reshape(n * x.shape[0], x.shape[1])


def add(a, *more):
    total = a.astype(f32)
    for x in more:
        total = total + x.astype(f32)
    return total.astype(bf16)


def body(queries, key_rows, value_rows, out_grads, doc_ids, owner_plan):
    n = NZ * NY
    me = lax.axis_index("ctx")
    rows, width = queries.shape
    pieces = jnp.arange(n, dtype=jnp.int32)
    my_owners = lax.dynamic_index_in_dim(owner_plan, me, 0, keepdims=False)

    r = jnp.arange(rows, dtype=jnp.int32)
    owner_row = jnp.repeat(my_owners, PIECE) * PIECE + r % PIECE
    onehot = (r[:, None] == owner_row[None, :]).astype(bf16)

    outgoing = jnp.dot(onehot, queries, preferred_element_type=f32).astype(bf16)
    q = lax.all_to_all(outgoing.reshape(n, PIECE, width), "ctx", 0, 0, tiled=True).reshape(rows, width)
    g = lax.all_to_all(out_grads, "head", split_axis=1, concat_axis=0, tiled=True)

    k_own = spread(key_rows, Y_GROUPS)
    ups, downs = [k_own], [k_own]
    for step in range(NZ // 2):
        ups.append(shift(ups[-1], 1, 0))
        if step < NZ // 2 - 1:
            downs.append(shift(downs[-1], -1, 0))
    ks = ups + downs[:0:-1]

    v_own = spread(value_rows, Z_GROUPS)
    v_up, v_down = shift(v_own, 0, 1), shift(v_own, 0, -1)
    half = v_own.shape[0] // 2
    vs = [v_own, v_up, v_down, shift(v_up[:half], 0, 1), shift(v_down[half:], 0, -1)]

    slot_of = jnp.sum(jnp.where(owner_plan == me, pieces[None, :], 0), axis=1)
    place = (
        pieces[:, None] * TOK + slot_of[:, None] * PIECE + jnp.arange(PIECE, dtype=jnp.int32)[None, :]
    ).reshape(GROUPS, 1, 1, rows // GROUPS)
    docs = jnp.arange(DOCS, dtype=jnp.int32)
    doc_first = jnp.sum((doc_ids[:, None] < docs[None, :]).astype(jnp.int32), axis=0)
    start = jnp.max(jnp.where(doc_first <= place[..., None], doc_first, 0), axis=-1)
    lo = jnp.min(start, axis=(1, 2, 3)) // KB
    hi = jnp.max(place, axis=(1, 2, 3)) // KB + 1
    spread_lanes = lambda x: jnp.broadcast_to(x, (GROUPS, 1, width // HD, rows // GROUPS)).reshape(GROUPS, 1, -1)
    at = jnp.stack([me // NY, me % NY])

    o, dq, dks, dvs = attend(lo, hi, at, spread_lanes(place), spread_lanes(start), q, g, ks, vs)

    returned = lax.all_to_all(dq.reshape(n, PIECE, width), "ctx", 0, 0, tiled=True).reshape(rows, width)
    attention = lax.all_to_all(o, "head", split_axis=0, concat_axis=1, tiled=True)

    up, down = dks[4], dks[5]
    up = add(dks[3], shift(up, 1, 0))
    for i in (2, 1):
        up = add(dks[i], shift(up, 1, 0))
        down = add(dks[8 - i], shift(down, -1, 0))
    k_sum = add(dks[0], shift(up, 1, 0), shift(down, -1, 0))
    key_grads = jnp.sum(swap(k_sum.reshape(NY, TOK, HD), Y_GROUPS).astype(f32), axis=0).astype(bf16)

    a_up = add(dvs[2], shift(dvs[4], 0, 1))
    b_down = add(dvs[7], shift(dvs[5], 0, -1))
    a_sum = add(dvs[0], shift(dvs[6], 0, -1), shift(a_up, 0, 1))
    b_sum = add(dvs[1], shift(dvs[3], 0, 1), shift(b_down, 0, -1))
    v_sum = jnp.concatenate([a_sum, b_sum], axis=0).reshape(NZ, TOK, HD)
    value_grads = jnp.sum(swap(v_sum, Z_GROUPS).astype(f32), axis=0).astype(bf16)

    query_grads = jnp.dot(onehot.T, returned, preferred_element_type=f32).astype(bf16)
    return attention, query_grads, key_grads, value_grads


def solution(mesh):
    return jax.shard_map(
        body,
        mesh=mesh,
        in_specs=(P("ctx", "head"),) * 3 + (P(("ctx", "head"), None), P(), P()),
        out_specs=(P(("ctx", "head"), None),) + (P("ctx", "head"),) * 3,
        check_vma=False,
    )
```

```python
import jax
import jax.numpy as jnp
from jax import lax
from jax.experimental import pallas as pl
from jax.experimental.pallas import tpu as pltpu
from jax.sharding import Mesh
from jax.sharding import PartitionSpec as P

HD = 128
NZ = 8
NY = 4
TOK = 256
PLANE = NY * TOK
PIECE = 8
DOCLEN = 4096
DOCS = 8
GROUPS = 8
MOST = DOCLEN // PLANE + 1
MASKED = -1e30
LOG2E = 1.4426950408889634
f32 = jnp.float32
bf16 = jnp.bfloat16


def attend_kernel(lo_ref, hi_ref, at_ref, place_ref, start_ref, q_ref, g_ref, *refs):
    own_refs, twin_refs = refs[:NZ], refs[NZ : 2 * NZ]
    refs = refs[2 * NZ :]
    o_ref, dq_ref = refs[:2]
    keep_refs, give_refs = refs[2 : 2 + NZ], refs[2 + NZ : 2 + 2 * NZ]
    kn, vn, kt, vt, dk_acc, dv_acc, s_ref, e_ref = refs[2 + 2 * NZ :]
    rows, width = q_ref.shape
    heads = width // HD
    span = rows // GROUPS
    lanes = span * heads
    scale = HD**-0.5
    half = PLANE // 2
    my_z = at_ref[0]

    for rz in range(NZ):
        z = lax.rem(my_z + NZ - rz, NZ)
        for part, refs_of in ((slice(0, half), own_refs), (slice(half, PLANE), twin_refs)):
            kn[z, part, :] = refs_of[rz][:, :HD]
            vn[z, part, :] = refs_of[rz][:, HD:]

    def prepare(b, carry):
        kt[b] = kn[b].T
        vt[b] = vn[b].T
        dk_acc[b] = jnp.zeros(dk_acc.shape[1:], f32)
        dv_acc[b] = jnp.zeros(dv_acc.shape[1:], f32)
        return carry

    lax.fori_loop(0, NZ, prepare, 0)

    def gather_heads(ref, at):
        x = ref[at, :]
        return jnp.concatenate([x[:, h * HD : (h + 1) * HD] for h in range(heads)], axis=0)

    def scatter_heads(ref, at, x):
        for h in range(heads):
            ref[at, h * HD : (h + 1) * HD] = x[h * span : (h + 1) * span]

    def group(gi, carry):
        at = pl.ds(pl.multiple_of(gi * span, span), span)
        lo, hi = lo_ref[gi], hi_ref[gi]
        place, start = place_ref[gi], start_ref[gi]
        qt = gather_heads(q_ref, at).astype(f32).T
        gt = gather_heads(g_ref, at).astype(f32).T
        qtb, gtb = qt.astype(bf16), gt.astype(bf16)

        def score(kb, peak):
            s = jnp.dot(kn[kb], qtb, preferred_element_type=f32)
            u = lax.broadcasted_iota(jnp.int32, (TOK, lanes), 0)
            for ry in range(NY):
                base = kb * PLANE + at_ref[1 + ry] * TOK
                part = s[ry * TOK : (ry + 1) * TOK]
                part = jnp.where((u >= start - base) & (u <= place - base), part, MASKED)
                s_ref[kb - lo, ry * TOK : (ry + 1) * TOK, :] = part
                peak = jnp.maximum(peak, jnp.max(part.reshape(TOK // 8, 8, lanes), axis=0))
            return peak

        peak = lax.fori_loop(lo, hi, score, jnp.full((8, lanes), MASKED, f32))
        peak = jnp.max(peak, axis=0, keepdims=True) * (scale * LOG2E)

        def weigh(kb, carry):
            ot, total = carry
            e = jnp.exp2(s_ref[kb - lo] * (scale * LOG2E) - peak)
            eb = e.astype(bf16)
            e_ref[kb - lo] = eb
            total = total + jnp.sum(e.reshape(-1, 8, lanes), axis=0)
            return ot + jnp.dot(vt[kb], eb, preferred_element_type=f32), total

        ot, total = lax.fori_loop(
            lo, hi, weigh, (jnp.zeros((HD, lanes), f32), jnp.zeros((8, lanes), f32))
        )
        inverse = 1.0 / jnp.sum(total, axis=0, keepdims=True)
        otb = (ot * inverse).astype(bf16).astype(f32)
        scatter_heads(o_ref, at, otb.T.astype(bf16))
        delta = jnp.sum(otb * gt, axis=0, keepdims=True)
        qs = (qt * inverse).T.astype(bf16)
        gs = (gt * inverse).T.astype(bf16)

        def back(kb, dqt):
            dp = jnp.dot(vn[kb], gtb, preferred_element_type=f32)
            eb = e_ref[kb - lo]
            ds = (eb.astype(f32) * (dp - delta)).astype(bf16)
            dk_acc[kb] += jnp.dot(ds, qs, preferred_element_type=f32)
            dv_acc[kb] += jnp.dot(eb, gs, preferred_element_type=f32)
            return dqt + jnp.dot(kt[kb], ds, preferred_element_type=f32)

        dqt = lax.fori_loop(lo, hi, back, jnp.zeros((HD, lanes), f32))
        scatter_heads(dq_ref, at, (dqt * (inverse * scale)).T.astype(bf16))
        return carry

    lax.fori_loop(0, GROUPS, group, 0)

    for rz in range(NZ):
        z = lax.rem(my_z + rz, NZ)
        for part, refs_of in ((slice(0, half), keep_refs), (slice(half, PLANE), give_refs)):
            refs_of[rz][:, :HD] = (dk_acc[z, part, :] * scale).astype(bf16)
            refs_of[rz][:, HD:] = dv_acc[z, part, :].astype(bf16)


def attend(lo, hi, at, place, start, q, g, own, twin):
    rows, width = q.shape
    lanes = rows // GROUPS * (width // HD)
    vm = pl.BlockSpec(memory_space=pltpu.VMEM)
    sm = pl.BlockSpec(memory_space=pltpu.SMEM)
    outs = (
        [jax.ShapeDtypeStruct((rows, width), bf16)] * 2
        + [jax.ShapeDtypeStruct((PLANE // 2, 2 * HD), bf16)] * (2 * NZ)
    )
    out = pl.pallas_call(
        attend_kernel,
        in_specs=[sm] * 3 + [vm] * (4 + 2 * NZ),
        out_specs=[vm] * len(outs),
        out_shape=outs,
        scratch_shapes=[
            pltpu.VMEM((NZ, PLANE, HD), bf16),
            pltpu.VMEM((NZ, PLANE, HD), bf16),
            pltpu.VMEM((NZ, HD, PLANE), bf16),
            pltpu.VMEM((NZ, HD, PLANE), bf16),
            pltpu.VMEM((NZ, PLANE, HD), f32),
            pltpu.VMEM((NZ, PLANE, HD), f32),
            pltpu.VMEM((MOST, PLANE, lanes), f32),
            pltpu.VMEM((MOST, PLANE, lanes), bf16),
        ],
        compiler_params=pltpu.CompilerParams(vmem_limit_bytes=52 * 1024 * 1024),
        cost_estimate=pl.CostEstimate(
            flops=12 * 10**9, bytes_accessed=12 * 10**6, transcendentals=4 * 10**6
        ),
        name="attend",
    )(lo, hi, at, place, start, q, g, *own, *twin)
    return out[0], out[1], out[2 : 2 + NZ], out[2 + NZ :]


AXES = ("z", "p", "b", "x", "c")
OWNER = ("z", "p", "c")
HEAD = ("x", "b")


def swap(x):
    return lax.ppermute(x, ("b", "c"), [(0, 0), (1, 2), (2, 1), (3, 3)])


def ring(x, step):
    return lax.ppermute(x, "z", [(i, (i + step) % NZ) for i in range(NZ)])


def twin(x):
    return lax.ppermute(x, "c", [(0, 1), (1, 0)])


def across(x):
    return lax.ppermute(x, "p", [(0, 1), (1, 0)])


def after(x, *others):
    return lax.optimization_barrier((x, others))[0]


def add(*terms):
    total = terms[0].astype(f32)
    for x in terms[1:]:
        total = total + x.astype(f32)
    return total.astype(bf16)


def body(queries, key_rows, value_rows, out_grads, doc_ids, owner_plan):
    n = NZ * NY
    me = lax.axis_index(OWNER)
    p, c = lax.axis_index("p"), lax.axis_index("c")
    rows, width = queries.shape
    pieces = jnp.arange(n, dtype=jnp.int32)
    my_owners = lax.dynamic_index_in_dim(owner_plan, me, 0, keepdims=False)

    mine = swap(jnp.concatenate([key_rows, value_rows], axis=1))
    home = swap(queries)
    mine = jnp.concatenate([mine, across(mine)], axis=0)

    r = jnp.arange(rows, dtype=jnp.int32)
    owner_row = jnp.repeat(my_owners, PIECE) * PIECE + r % PIECE
    onehot = (r[:, None] == owner_row[None, :]).astype(bf16)
    outgoing = jnp.dot(onehot, home, preferred_element_type=f32).astype(bf16)

    q = lax.all_to_all(outgoing.reshape(n, PIECE, width), OWNER, 0, 0, tiled=True).reshape(rows, width)
    g = lax.all_to_all(after(swap(out_grads), q), HEAD, split_axis=1, concat_axis=0, tiled=True)

    ups, downs = [mine], [mine]
    for step in range(NZ // 2):
        ups.append(ring(ups[-1], 1))
        if step < NZ // 2 - 1:
            downs.append(ring(downs[-1], -1))
    own = ups + downs[:0:-1]
    twins = [twin(x) for x in own]

    slot_of = jnp.sum(jnp.where(owner_plan == me, pieces[None, :], 0), axis=1)
    place = (
        pieces[:, None] * TOK + slot_of[:, None] * PIECE + jnp.arange(PIECE, dtype=jnp.int32)[None, :]
    ).reshape(GROUPS, 1, 1, rows // GROUPS)
    docs = jnp.arange(DOCS, dtype=jnp.int32)
    doc_first = jnp.sum((doc_ids[:, None] < docs[None, :]).astype(jnp.int32), axis=0)
    start = jnp.max(jnp.where(doc_first <= place[..., None], doc_first, 0), axis=-1)
    lo = jnp.min(start, axis=(1, 2, 3)) // PLANE
    hi = jnp.max(place, axis=(1, 2, 3)) // PLANE + 1
    spread_lanes = lambda x: jnp.broadcast_to(x, (GROUPS, 1, width // HD, rows // GROUPS)).reshape(GROUPS, 1, -1)
    at = jnp.stack([me // NY] + [2 * (p ^ (j & 1)) + (c ^ (j >> 1)) for j in range(NY)])

    o, dq, keep, give = attend(lo, hi, at, spread_lanes(place), spread_lanes(start), q, g, own, twins)

    got = [None] * NZ
    for r in (4, 5, 3, 6, 2, 7, 1, 0):
        got[r] = twin(give[r])
    up = ring(add(keep[4], got[4]), 1)
    down = ring(add(keep[5], got[5]), -1)
    for r in (3, 2, 1):
        up = ring(add(keep[r], got[r], up), 1)
        if r > 1:
            down = ring(add(keep[9 - r], got[9 - r], down), -1)
    total = [x.astype(f32) for x in (keep[0], got[0], up, down)]
    total = total[0] + total[1] + total[2] + total[3]
    other = across(total[TOK:].astype(bf16))
    grads = swap((total[:TOK] + other.astype(f32)).astype(bf16))

    returned = lax.all_to_all(dq.reshape(n, PIECE, width), OWNER, 0, 0, tiled=True).reshape(rows, width)
    attention = lax.all_to_all(after(o, returned), HEAD, split_axis=0, concat_axis=1, tiled=True)
    query_grads = jnp.dot(onehot.T, returned, preferred_element_type=f32).astype(bf16)
    return swap(attention), swap(query_grads), grads[:, :HD], grads[:, HD:]


def solution(mesh):
    ctx, head = ("z", "p", "b"), ("x", "c")
    fine = Mesh(mesh.devices.reshape(NZ, 2, 2, -1, 2), AXES)
    rows = P(ctx + head, None)
    return jax.shard_map(
        body,
        mesh=fine,
        in_specs=(P(ctx, head),) * 3 + (rows, P(), P()),
        out_specs=(rows,) + (P(ctx, head),) * 3,
        check_vma=False,
    )
```

```python
import jax
import jax.numpy as jnp
from jax import lax
from jax.experimental import pallas as pl
from jax.experimental.pallas import tpu as pltpu
from jax.sharding import Mesh
from jax.sharding import PartitionSpec as P

HD = 128
NZ = 8
NY = 4
TOK = 256
PLANE = NY * TOK
PIECE = 8
DOCLEN = 4096
DOCS = 8
GROUPS = 8
MOST = DOCLEN // PLANE + 1
MASKED = -1e30
LOG2E = 1.4426950408889634
f32 = jnp.float32
bf16 = jnp.bfloat16


def attend_kernel(lo_ref, hi_ref, at_ref, place_ref, start_ref, q_ref, g_ref, *refs):
    own_refs, twin_refs = refs[:NZ], refs[NZ : 2 * NZ]
    refs = refs[2 * NZ :]
    o_ref, dq_ref = refs[:2]
    keep_refs, give_refs = refs[2 : 2 + NZ], refs[2 + NZ : 2 + 2 * NZ]
    kn, vn, kt, vt, dk_acc, dv_acc, s_ref, e_ref = refs[2 + 2 * NZ :]
    rows, width = q_ref.shape
    heads = width // HD
    span = rows // GROUPS
    lanes = span * heads
    scale = HD**-0.5
    half = PLANE // 2
    my_z = at_ref[0]

    for rz in range(NZ):
        z = lax.rem(my_z + NZ - rz, NZ)
        for part, refs_of in ((slice(0, half), own_refs), (slice(half, PLANE), twin_refs)):
            kn[z, part, :] = refs_of[rz][:, :HD]
            vn[z, part, :] = refs_of[rz][:, HD:]

    def prepare(b, carry):
        kt[b] = kn[b].T
        vt[b] = vn[b].T
        dk_acc[b] = jnp.zeros(dk_acc.shape[1:], f32)
        dv_acc[b] = jnp.zeros(dv_acc.shape[1:], f32)
        return carry

    lax.fori_loop(0, NZ, prepare, 0)

    def gather_heads(ref, at):
        x = ref[at, :]
        return jnp.concatenate([x[:, h * HD : (h + 1) * HD] for h in range(heads)], axis=0)

    def scatter_heads(ref, at, x):
        for h in range(heads):
            ref[at, h * HD : (h + 1) * HD] = x[h * span : (h + 1) * span]

    def group(gi, carry):
        at = pl.ds(pl.multiple_of(gi * span, span), span)
        lo, hi = lo_ref[gi], hi_ref[gi]
        place, start = place_ref[gi], start_ref[gi]
        qt = gather_heads(q_ref, at).astype(f32).T
        gt = gather_heads(g_ref, at).astype(f32).T
        qtb, gtb = qt.astype(bf16), gt.astype(bf16)

        def score(kb, peak):
            s = jnp.dot(kn[kb], qtb, preferred_element_type=f32)
            u = lax.broadcasted_iota(jnp.int32, (TOK, lanes), 0)
            for ry in range(NY):
                base = kb * PLANE + at_ref[1 + ry] * TOK
                part = s[ry * TOK : (ry + 1) * TOK]
                part = jnp.where((u >= start - base) & (u <= place - base), part, MASKED)
                s_ref[kb - lo, ry * TOK : (ry + 1) * TOK, :] = part
                peak = jnp.maximum(peak, jnp.max(part.reshape(TOK // 8, 8, lanes), axis=0))
            return peak

        peak = lax.fori_loop(lo, hi, score, jnp.full((8, lanes), MASKED, f32))
        peak = jnp.max(peak, axis=0, keepdims=True) * (scale * LOG2E)

        def weigh(kb, carry):
            ot, total = carry
            e = jnp.exp2(s_ref[kb - lo] * (scale * LOG2E) - peak)
            eb = e.astype(bf16)
            e_ref[kb - lo] = eb
            total = total + jnp.sum(e.reshape(-1, 8, lanes), axis=0)
            return ot + jnp.dot(vt[kb], eb, preferred_element_type=f32), total

        ot, total = lax.fori_loop(
            lo, hi, weigh, (jnp.zeros((HD, lanes), f32), jnp.zeros((8, lanes), f32))
        )
        inverse = 1.0 / jnp.sum(total, axis=0, keepdims=True)
        otb = (ot * inverse).astype(bf16).astype(f32)
        scatter_heads(o_ref, at, otb.T.astype(bf16))
        delta = jnp.sum(otb * gt, axis=0, keepdims=True)
        qs = (qt * inverse).T.astype(bf16)
        gs = (gt * inverse).T.astype(bf16)

        def back(kb, dqt):
            dp = jnp.dot(vn[kb], gtb, preferred_element_type=f32)
            eb = e_ref[kb - lo]
            ds = (eb.astype(f32) * (dp - delta)).astype(bf16)
            dk_acc[kb] += jnp.dot(ds, qs, preferred_element_type=f32)
            dv_acc[kb] += jnp.dot(eb, gs, preferred_element_type=f32)
            return dqt + jnp.dot(kt[kb], ds, preferred_element_type=f32)

        dqt = lax.fori_loop(lo, hi, back, jnp.zeros((HD, lanes), f32))
        scatter_heads(dq_ref, at, (dqt * (inverse * scale)).T.astype(bf16))
        return carry

    lax.fori_loop(0, GROUPS, group, 0)

    for rz in range(NZ):
        z = lax.rem(my_z + rz, NZ)
        for part, refs_of in ((slice(0, half), keep_refs), (slice(half, PLANE), give_refs)):
            refs_of[rz][:, :HD] = (dk_acc[z, part, :] * scale).astype(bf16)
            refs_of[rz][:, HD:] = dv_acc[z, part, :].astype(bf16)


def attend(lo, hi, at, place, start, q, g, own, twin):
    rows, width = q.shape
    lanes = rows // GROUPS * (width // HD)
    vm = pl.BlockSpec(memory_space=pltpu.VMEM)
    sm = pl.BlockSpec(memory_space=pltpu.SMEM)
    outs = (
        [jax.ShapeDtypeStruct((rows, width), bf16)] * 2
        + [jax.ShapeDtypeStruct((PLANE // 2, 2 * HD), bf16)] * (2 * NZ)
    )
    out = pl.pallas_call(
        attend_kernel,
        in_specs=[sm] * 3 + [vm] * (4 + 2 * NZ),
        out_specs=[vm] * len(outs),
        out_shape=outs,
        scratch_shapes=[
            pltpu.VMEM((NZ, PLANE, HD), bf16),
            pltpu.VMEM((NZ, PLANE, HD), bf16),
            pltpu.VMEM((NZ, HD, PLANE), bf16),
            pltpu.VMEM((NZ, HD, PLANE), bf16),
            pltpu.VMEM((NZ, PLANE, HD), f32),
            pltpu.VMEM((NZ, PLANE, HD), f32),
            pltpu.VMEM((MOST, PLANE, lanes), f32),
            pltpu.VMEM((MOST, PLANE, lanes), bf16),
        ],
        compiler_params=pltpu.CompilerParams(vmem_limit_bytes=52 * 1024 * 1024),
        cost_estimate=pl.CostEstimate(
            flops=12 * 10**9, bytes_accessed=12 * 10**6, transcendentals=4 * 10**6
        ),
        name="attend",
    )(lo, hi, at, place, start, q, g, *own, *twin)
    return out[0], out[1], out[2 : 2 + NZ], out[2 + NZ :]


AXES = ("z", "p", "b", "x", "c")
OWNER = ("z", "p", "c")


def swap(x):
    return lax.ppermute(x, ("b", "c"), [(0, 0), (1, 2), (2, 1), (3, 3)])


def ring(x, step):
    return lax.ppermute(x, "z", [(i, (i + step) % NZ) for i in range(NZ)])


def twin(x):
    return lax.ppermute(x, "c", [(0, 1), (1, 0)])


def swap_across(x):
    pairs = [(4 * p + 2 * b + c, 4 * (1 - p) + 2 * c + b) for p in range(2) for b in range(2) for c in range(2)]
    return lax.ppermute(x, ("p", "b", "c"), pairs)


def nothing(x):
    return x[0, 0].astype(f32) * 0.0


def add(*terms):
    total = terms[0].astype(f32)
    for x in terms[1:]:
        total = total + x.astype(f32)
    return total.astype(bf16)


def body(queries, key_rows, value_rows, out_grads, doc_ids, owner_plan):
    n = NZ * NY
    me = lax.axis_index(OWNER)
    p, c = lax.axis_index("p"), lax.axis_index("c")
    rows, width = queries.shape
    pieces = jnp.arange(n, dtype=jnp.int32)
    owners = lax.dynamic_index_in_dim(owner_plan, me, 0, keepdims=False)

    r = jnp.arange(rows, dtype=jnp.int32)
    owner_row = jnp.repeat(owners, PIECE) * PIECE + r % PIECE
    onehot = (r[:, None] == owner_row[None, :]).astype(bf16)
    outgoing = jnp.dot(onehot, swap(queries), preferred_element_type=f32).astype(bf16)
    q = lax.all_to_all(outgoing.reshape(n, PIECE, width), OWNER, 0, 0, tiled=True).reshape(rows, width)
    g = lax.all_to_all(out_grads, ("x", "c"), split_axis=1, concat_axis=0, tiled=True)
    g = swap(g)

    mine = jnp.concatenate([key_rows, value_rows], axis=1)
    mine = jnp.concatenate([swap(mine), swap_across(mine)], axis=0)
    ups, downs = [mine], [mine]
    for step in range(NZ // 2):
        ups.append(ring(ups[-1], 1))
        if step < NZ // 2 - 1:
            downs.append(ring(downs[-1], -1))
    own = ups + downs[:0:-1]
    twins = [twin(x) for x in own]

    slot_of = jnp.sum(jnp.where(owner_plan == me, pieces[None, :], 0), axis=1)
    place = (
        pieces[:, None] * TOK + slot_of[:, None] * PIECE + jnp.arange(PIECE, dtype=jnp.int32)[None, :]
    ).reshape(GROUPS, 1, 1, rows // GROUPS)
    docs = jnp.arange(DOCS, dtype=jnp.int32)
    doc_first = jnp.sum((doc_ids[:, None] < docs[None, :]).astype(jnp.int32), axis=0)
    start = jnp.max(jnp.where(doc_first <= place[..., None], doc_first, 0), axis=-1)
    lo = jnp.min(start, axis=(1, 2, 3)) // PLANE
    hi = jnp.max(place, axis=(1, 2, 3)) // PLANE + 1
    spread_lanes = lambda x: jnp.broadcast_to(x, (GROUPS, 1, width // HD, rows // GROUPS)).reshape(GROUPS, 1, -1)
    at = jnp.stack([me // NY] + [2 * (p ^ (j & 1)) + (c ^ (j >> 1)) for j in range(NY)])

    o, dq, keep, give = attend(lo, hi, at, spread_lanes(place), spread_lanes(start), q, g, own, twins)

    returned = lax.all_to_all(dq.reshape(n, PIECE, width), OWNER, 0, 0, tiled=True).reshape(rows, width)
    o = swap(o)
    attention = lax.all_to_all(add(o, nothing(returned)), ("x", "c"), split_axis=0, concat_axis=1, tiled=True)
    query_grads = swap(jnp.dot(onehot.T, returned, preferred_element_type=f32).astype(bf16))

    got = [None] * NZ
    for r in (4, 5, 3, 6, 2, 7, 1, 0):
        got[r] = twin(give[r])
    up = ring(add(keep[4], got[4]), 1)
    down = ring(add(keep[5], got[5]), -1)
    for r in (3, 2, 1):
        up = ring(add(keep[r], got[r], up, *([nothing(o)] if r == 2 else [])), 1)
        if r > 1:
            down = ring(add(keep[9 - r], got[9 - r], down), -1)
    total = add(keep[0], got[0], up, down, nothing(query_grads))
    grads = add(swap(total[:TOK]), swap_across(total[TOK:]))

    return attention, query_grads, grads[:, :HD], grads[:, HD:]


def solution(mesh):
    ctx, head = ("z", "p", "b"), ("x", "c")
    fine = Mesh(mesh.devices.reshape(NZ, 2, 2, -1, 2), AXES)
    rows = P(ctx + head, None)
    return jax.shard_map(
        body,
        mesh=fine,
        in_specs=(P(ctx, head),) * 3 + (rows, P(), P()),
        out_specs=(rows,) + (P(ctx, head),) * 3,
        check_vma=False,
    )
```

```python
import jax
import jax.numpy as jnp
from jax import lax
from jax.experimental import pallas as pl
from jax.experimental.pallas import tpu as pltpu
from jax.sharding import Mesh
from jax.sharding import PartitionSpec as P

HD = 128
NZ = 8
NY = 4
TOK = 256
PLANE = NY * TOK
PIECE = 8
DOCLEN = 4096
DOCS = 8
GROUPS = 8
MOST = DOCLEN // PLANE + 1
MASKED = -1e30
LOG2E = 1.4426950408889634
f32 = jnp.float32
bf16 = jnp.bfloat16


def attend_kernel(lo_ref, hi_ref, at_ref, place_ref, start_ref, q_ref, g_ref, *refs):
    own_refs, twin_refs = refs[:NZ], refs[NZ : 2 * NZ]
    refs = refs[2 * NZ :]
    o_ref, dq_ref = refs[:2]
    keep_refs, give_refs = refs[2 : 2 + NZ], refs[2 + NZ : 2 + 2 * NZ]
    kn, vn, dk_acc, dv_acc, s_ref, e_ref = refs[2 + 2 * NZ :]
    rows, width = q_ref.shape
    heads = width // HD
    span = rows // GROUPS
    lanes = span * heads
    scale = HD**-0.5
    half = PLANE // 2
    my_z = at_ref[0]

    for rz in range(NZ):
        z = lax.rem(my_z + NZ - rz, NZ)
        for part, refs_of in ((slice(0, half), own_refs), (slice(half, PLANE), twin_refs)):
            kn[z, part, :] = refs_of[rz][:, :HD]
            vn[z, part, :] = refs_of[rz][:, HD:]

    def gather_heads(ref, at):
        x = ref[at, :]
        return jnp.concatenate([x[:, h * HD : (h + 1) * HD] for h in range(heads)], axis=0)

    def scatter_heads(ref, at, x):
        for h in range(heads):
            ref[at, h * HD : (h + 1) * HD] = x[h * span : (h + 1) * span]

    ones = jnp.ones((8, PLANE), bf16)

    def score(kb, slot, own_plane, qt, place, start, peak):
        s = jnp.dot(kn[kb], qt, preferred_element_type=f32)
        u = lax.broadcasted_iota(jnp.int32, (TOK, lanes), 0)
        for ry in range(NY):
            base = kb * PLANE + at_ref[1 + ry] * TOK
            part = s[ry * TOK : (ry + 1) * TOK]
            seen = u >= start - base
            if own_plane:
                seen = seen & (u <= place - base)
            part = jnp.where(seen, part, MASKED)
            s_ref[slot, ry * TOK : (ry + 1) * TOK, :] = part
            peak = jnp.maximum(peak, jnp.max(part.reshape(TOK // 8, 8, lanes), axis=0))
        return peak

    def weigh(kb, slot, peak, ot, total):
        e = jnp.exp2(s_ref[slot] * (scale * LOG2E) - peak)
        eb = e.astype(bf16)
        e_ref[slot] = eb
        total = total + jnp.dot(ones, eb, preferred_element_type=f32)
        return ot + lax.dot_general(vn[kb], eb, (((0,), (0,)), ((), ())), preferred_element_type=f32), total

    def back(kb, slot, own_plane, gt, delta, qs, gs, dqt):
        dp = jnp.dot(vn[kb], gt, preferred_element_type=f32)
        eb = e_ref[slot]
        ds = (eb.astype(f32) * (dp - delta)).astype(bf16)
        dk = jnp.dot(ds, qs, preferred_element_type=f32)
        dv = jnp.dot(eb, gs, preferred_element_type=f32)
        if own_plane:
            dk_acc[kb] = dk
            dv_acc[kb] = dv
        else:
            dk_acc[kb] += dk
            dv_acc[kb] += dv
        return dqt + lax.dot_general(kn[kb], ds, (((0,), (0,)), ((), ())), preferred_element_type=f32)

    def begin(gi):
        at = pl.ds(gi * span, span)
        place, start = place_ref[gi], start_ref[gi]
        qt = gather_heads(q_ref, at).astype(f32).T
        gt = gather_heads(g_ref, at).astype(f32).T
        peak = score(gi, 0, True, qt.astype(bf16), place, start, jnp.full((8, lanes), MASKED, f32))
        return qt, gt, place, start, peak

    begun = begin(0)
    for gi in range(GROUPS):
        at = pl.ds(gi * span, span)
        lo = lo_ref[gi]
        qt, gt, place, start, peak = begun
        qtb, gtb = qt.astype(bf16), gt.astype(bf16)
        peak = lax.fori_loop(
            lo, gi, lambda kb, x: score(kb, 1 + kb - lo, False, qtb, place, start, x), peak
        )
        peak = jnp.max(peak, axis=0, keepdims=True) * (scale * LOG2E)

        zero = (jnp.zeros((HD, lanes), f32), jnp.zeros((8, lanes), f32))
        ot, total = lax.fori_loop(
            lo, gi, lambda kb, x: weigh(kb, 1 + kb - lo, peak, *x), weigh(gi, 0, peak, *zero)
        )
        inverse = 1.0 / total[:1]
        otb = (ot * inverse).astype(bf16).astype(f32)
        scatter_heads(o_ref, at, otb.T.astype(bf16))
        delta = jnp.sum(otb * gt, axis=0, keepdims=True)
        qs = (qt * inverse).T.astype(bf16)
        gs = (gt * inverse).T.astype(bf16)

        dqt = lax.fori_loop(
            lo, gi, lambda kb, x: back(kb, 1 + kb - lo, False, gtb, delta, qs, gs, x), jnp.zeros((HD, lanes), f32)
        )
        dqt = back(gi, 0, True, gtb, delta, qs, gs, dqt)
        if gi + 1 < GROUPS:
            begun = begin(gi + 1)
        scatter_heads(dq_ref, at, (dqt * (inverse * scale)).T.astype(bf16))

    for rz in range(NZ):
        z = lax.rem(my_z + rz, NZ)
        for part, refs_of in ((slice(0, half), keep_refs), (slice(half, PLANE), give_refs)):
            refs_of[rz][:, :HD] = (dk_acc[z, part, :] * scale).astype(bf16)
            refs_of[rz][:, HD:] = dv_acc[z, part, :].astype(bf16)


def attend(lo, hi, at, place, start, q, g, own, twin):
    rows, width = q.shape
    lanes = rows // GROUPS * (width // HD)
    vm = pl.BlockSpec(memory_space=pltpu.VMEM)
    sm = pl.BlockSpec(memory_space=pltpu.SMEM)
    outs = (
        [jax.ShapeDtypeStruct((rows, width), bf16)] * 2
        + [jax.ShapeDtypeStruct((PLANE // 2, 2 * HD), bf16)] * (2 * NZ)
    )
    out = pl.pallas_call(
        attend_kernel,
        in_specs=[sm] * 3 + [vm] * (4 + 2 * NZ),
        out_specs=[vm] * len(outs),
        out_shape=outs,
        scratch_shapes=[
            pltpu.VMEM((NZ, PLANE, HD), bf16),
            pltpu.VMEM((NZ, PLANE, HD), bf16),
            pltpu.VMEM((NZ, PLANE, HD), f32),
            pltpu.VMEM((NZ, PLANE, HD), f32),
            pltpu.VMEM((MOST, PLANE, lanes), f32),
            pltpu.VMEM((MOST, PLANE, lanes), bf16),
        ],
        compiler_params=pltpu.CompilerParams(vmem_limit_bytes=52 * 1024 * 1024),
        cost_estimate=pl.CostEstimate(
            flops=12 * 10**9, bytes_accessed=12 * 10**6, transcendentals=4 * 10**6
        ),
        name="attend",
    )(lo, hi, at, place, start, q, g, *own, *twin)
    return out[0], out[1], out[2 : 2 + NZ], out[2 + NZ :]


AXES = ("z", "p", "b", "x", "c")
OWNER = ("z", "p", "c")


def swap(x):
    return lax.ppermute(x, ("b", "c"), [(0, 0), (1, 2), (2, 1), (3, 3)])


def ring(x, step):
    return lax.ppermute(x, "z", [(i, (i + step) % NZ) for i in range(NZ)])


def twin(x):
    return lax.ppermute(x, "c", [(0, 1), (1, 0)])


def swap_across(x):
    pairs = [(4 * p + 2 * b + c, 4 * (1 - p) + 2 * c + b) for p in range(2) for b in range(2) for c in range(2)]
    return lax.ppermute(x, ("p", "b", "c"), pairs)


def nothing(x):
    return x[0, 0].astype(f32) * 0.0


def add(*terms):
    total = terms[0].astype(f32)
    for x in terms[1:]:
        total = total + x.astype(f32)
    return total.astype(bf16)


def body(queries, key_rows, value_rows, out_grads, doc_ids, owner_plan):
    n = NZ * NY
    me = lax.axis_index(OWNER)
    p, c = lax.axis_index("p"), lax.axis_index("c")
    rows, width = queries.shape
    pieces = jnp.arange(n, dtype=jnp.int32)
    owners = lax.dynamic_index_in_dim(owner_plan, me, 0, keepdims=False)

    r = jnp.arange(rows, dtype=jnp.int32)
    owner_row = jnp.repeat(owners, PIECE) * PIECE + r % PIECE
    onehot = (r[:, None] == owner_row[None, :]).astype(bf16)
    outgoing = jnp.dot(onehot, swap(queries), preferred_element_type=f32).astype(bf16)
    q = lax.all_to_all(outgoing.reshape(n, PIECE, width), OWNER, 0, 0, tiled=True).reshape(rows, width)
    g = lax.all_to_all(out_grads, ("x", "c"), split_axis=1, concat_axis=0, tiled=True)
    g = swap(g)

    mine = jnp.concatenate([key_rows, value_rows], axis=1)
    mine = jnp.concatenate([swap(mine), swap_across(mine)], axis=0)
    ups, downs = [mine], [mine]
    for step in range(NZ // 2):
        ups.append(ring(ups[-1], 1))
        if step < NZ // 2 - 1:
            downs.append(ring(downs[-1], -1))
    own = ups + downs[:0:-1]
    twins = [twin(x) for x in own]

    slot_of = jnp.sum(jnp.where(owner_plan == me, pieces[None, :], 0), axis=1)
    place = (
        pieces[:, None] * TOK + slot_of[:, None] * PIECE + jnp.arange(PIECE, dtype=jnp.int32)[None, :]
    ).reshape(GROUPS, 1, 1, rows // GROUPS)
    docs = jnp.arange(DOCS, dtype=jnp.int32)
    doc_first = jnp.sum((doc_ids[:, None] < docs[None, :]).astype(jnp.int32), axis=0)
    start = jnp.max(jnp.where(doc_first <= place[..., None], doc_first, 0), axis=-1)
    lo = jnp.min(start, axis=(1, 2, 3)) // PLANE
    hi = jnp.max(place, axis=(1, 2, 3)) // PLANE + 1
    spread_lanes = lambda x: jnp.broadcast_to(x, (GROUPS, 1, width // HD, rows // GROUPS)).reshape(GROUPS, 1, -1)
    at = jnp.stack([me // NY] + [2 * (p ^ (j & 1)) + (c ^ (j >> 1)) for j in range(NY)])

    o, dq, keep, give = attend(lo, hi, at, spread_lanes(place), spread_lanes(start), q, g, own, twins)

    returned = lax.all_to_all(dq.reshape(n, PIECE, width), OWNER, 0, 0, tiled=True).reshape(rows, width)
    o = swap(o)
    attention = lax.all_to_all(add(o, nothing(returned)), ("x", "c"), split_axis=0, concat_axis=1, tiled=True)
    query_grads = swap(jnp.dot(onehot.T, returned, preferred_element_type=f32).astype(bf16))

    got = [None] * NZ
    for r in (4, 5, 3, 6, 2, 7, 1, 0):
        got[r] = twin(give[r])
    up = ring(add(keep[4], got[4]), 1)
    down = ring(add(keep[5], got[5]), -1)
    for r in (3, 2, 1):
        up = ring(add(keep[r], got[r], up, *([nothing(o)] if r == 2 else [])), 1)
        if r > 1:
            down = ring(add(keep[9 - r], got[9 - r], down), -1)
    total = add(keep[0], got[0], up, down, nothing(query_grads))
    grads = add(swap(total[:TOK]), swap_across(total[TOK:]))

    return attention, query_grads, grads[:, :HD], grads[:, HD:]


def solution(mesh):
    ctx, head = ("z", "p", "b"), ("x", "c")
    fine = Mesh(mesh.devices.reshape(NZ, 2, 2, -1, 2), AXES)
    rows = P(ctx + head, None)
    return jax.shard_map(
        body,
        mesh=fine,
        in_specs=(P(ctx, head),) * 3 + (rows, P(), P()),
        out_specs=(rows,) + (P(ctx, head),) * 3,
        check_vma=False,
    )
```

```python
import jax
import jax.numpy as jnp
from jax import lax
from jax.experimental import pallas as pl
from jax.experimental.pallas import tpu as pltpu
from jax.sharding import Mesh
from jax.sharding import PartitionSpec as P

HD = 128
NZ = 8
NY = 4
TOK = 256
PLANE = NY * TOK
PIECE = 8
DOCLEN = 4096
DOCS = 8
GROUPS = 8
MOST = DOCLEN // PLANE + 1
MASKED = -1e30
LOG2E = 1.4426950408889634
f32 = jnp.float32
bf16 = jnp.bfloat16


def attend_kernel(lo_ref, hi_ref, at_ref, place_ref, start_ref, q_ref, g_ref, *refs):
    own_refs, twin_refs = refs[:NZ], refs[NZ : 2 * NZ]
    refs = refs[2 * NZ :]
    o_ref, dq_ref = refs[:2]
    keep_refs, give_refs = refs[2 : 2 + NZ], refs[2 + NZ : 2 + 2 * NZ]
    kn, vn, dk_acc, dv_acc, s_ref, e_ref = refs[2 + 2 * NZ :]
    rows, width = q_ref.shape
    heads = width // HD
    span = rows // GROUPS
    lanes = span * heads
    scale = HD**-0.5
    half = PLANE // 2
    my_z = at_ref[0]

    for rz in range(NZ):
        z = lax.rem(my_z + NZ - rz, NZ)
        for part, refs_of in ((slice(0, half), own_refs), (slice(half, PLANE), twin_refs)):
            kn[z, part, :] = refs_of[rz][:, :HD]
            vn[z, part, :] = refs_of[rz][:, HD:]

    def gather_heads(ref, at):
        x = ref[at, :]
        return jnp.concatenate([x[:, h * HD : (h + 1) * HD] for h in range(heads)], axis=0)

    def scatter_heads(ref, at, x):
        for h in range(heads):
            ref[at, h * HD : (h + 1) * HD] = x[h * span : (h + 1) * span]

    ones = jnp.ones((8, PLANE), bf16)

    def score(kb, slot, own_plane, qt, place, start, peak):
        s = jnp.dot(kn[kb], qt, preferred_element_type=f32)
        u = lax.broadcasted_iota(jnp.int32, (TOK, lanes), 0)
        for ry in range(NY):
            base = kb * PLANE + at_ref[1 + ry] * TOK
            part = s[ry * TOK : (ry + 1) * TOK]
            seen = u >= start - base
            if own_plane:
                seen = seen & (u <= place - base)
            part = jnp.where(seen, part, MASKED)
            s_ref[slot, ry * TOK : (ry + 1) * TOK, :] = part
            peak = jnp.maximum(peak, jnp.max(part.reshape(TOK // 8, 8, lanes), axis=0))
        return peak

    def weigh(kb, slot, peak, ot, total):
        e = jnp.exp2(s_ref[slot] * (scale * LOG2E) - peak)
        eb = e.astype(bf16)
        e_ref[slot] = eb
        total = total + jnp.dot(ones, eb, preferred_element_type=f32)
        return ot + lax.dot_general(vn[kb], eb, (((0,), (0,)), ((), ())), preferred_element_type=f32), total

    def back(kb, slot, own_plane, gt, delta, qs, gs, dqt):
        dp = jnp.dot(vn[kb], gt, preferred_element_type=f32)
        eb = e_ref[slot]
        ds = (eb.astype(f32) * (dp - delta)).astype(bf16)
        dk = jnp.dot(ds, qs, preferred_element_type=f32)
        dv = jnp.dot(eb, gs, preferred_element_type=f32)
        if own_plane:
            dk_acc[kb] = dk
            dv_acc[kb] = dv
        else:
            dk_acc[kb] += dk
            dv_acc[kb] += dv
        return dqt + lax.dot_general(kn[kb], ds, (((0,), (0,)), ((), ())), preferred_element_type=f32)

    def group(gi, carry):
        at = pl.ds(pl.multiple_of(gi * span, span), span)
        lo = lo_ref[gi]
        place, start = place_ref[gi], start_ref[gi]
        qt = gather_heads(q_ref, at).astype(f32).T
        gt = gather_heads(g_ref, at).astype(f32).T
        qtb, gtb = qt.astype(bf16), gt.astype(bf16)

        peak = score(gi, 0, True, qtb, place, start, jnp.full((8, lanes), MASKED, f32))
        peak = lax.fori_loop(
            lo, gi, lambda kb, x: score(kb, 1 + kb - lo, False, qtb, place, start, x), peak
        )
        peak = jnp.max(peak, axis=0, keepdims=True) * (scale * LOG2E)

        zero = (jnp.zeros((HD, lanes), f32), jnp.zeros((8, lanes), f32))
        ot, total = lax.fori_loop(
            lo, gi, lambda kb, x: weigh(kb, 1 + kb - lo, peak, *x), weigh(gi, 0, peak, *zero)
        )
        inverse = 1.0 / total[:1]
        otb = (ot * inverse).astype(bf16).astype(f32)
        scatter_heads(o_ref, at, otb.T.astype(bf16))
        delta = jnp.sum(otb * gt, axis=0, keepdims=True)
        qs = (qt * inverse).T.astype(bf16)
        gs = (gt * inverse).T.astype(bf16)

        dqt = back(gi, 0, True, gtb, delta, qs, gs, jnp.zeros((HD, lanes), f32))
        dqt = lax.fori_loop(
            lo, gi, lambda kb, x: back(kb, 1 + kb - lo, False, gtb, delta, qs, gs, x), dqt
        )
        scatter_heads(dq_ref, at, (dqt * (inverse * scale)).T.astype(bf16))
        return carry

    lax.fori_loop(0, GROUPS, group, 0)

    for rz in range(NZ):
        z = lax.rem(my_z + rz, NZ)
        for part, refs_of in ((slice(0, half), keep_refs), (slice(half, PLANE), give_refs)):
            refs_of[rz][:, :HD] = (dk_acc[z, part, :] * scale).astype(bf16)
            refs_of[rz][:, HD:] = dv_acc[z, part, :].astype(bf16)


def attend(lo, hi, at, place, start, q, g, own, twin):
    rows, width = q.shape
    lanes = rows // GROUPS * (width // HD)
    vm = pl.BlockSpec(memory_space=pltpu.VMEM)
    sm = pl.BlockSpec(memory_space=pltpu.SMEM)
    outs = (
        [jax.ShapeDtypeStruct((rows, width), bf16)] * 2
        + [jax.ShapeDtypeStruct((PLANE // 2, 2 * HD), bf16)] * (2 * NZ)
    )
    out = pl.pallas_call(
        attend_kernel,
        in_specs=[sm] * 3 + [vm] * (4 + 2 * NZ),
        out_specs=[vm] * len(outs),
        out_shape=outs,
        scratch_shapes=[
            pltpu.VMEM((NZ, PLANE, HD), bf16),
            pltpu.VMEM((NZ, PLANE, HD), bf16),
            pltpu.VMEM((NZ, PLANE, HD), f32),
            pltpu.VMEM((NZ, PLANE, HD), f32),
            pltpu.VMEM((MOST, PLANE, lanes), f32),
            pltpu.VMEM((MOST, PLANE, lanes), bf16),
        ],
        compiler_params=pltpu.CompilerParams(vmem_limit_bytes=52 * 1024 * 1024),
        cost_estimate=pl.CostEstimate(
            flops=12 * 10**9, bytes_accessed=12 * 10**6, transcendentals=4 * 10**6
        ),
        name="attend",
    )(lo, hi, at, place, start, q, g, *own, *twin)
    return out[0], out[1], out[2 : 2 + NZ], out[2 + NZ :]


AXES = ("z", "p", "b", "x", "c")
OWNER = ("z", "p", "c")


def swap(x):
    return lax.ppermute(x, ("b", "c"), [(0, 0), (1, 2), (2, 1), (3, 3)])


def ring(x, step):
    return lax.ppermute(x, "z", [(i, (i + step) % NZ) for i in range(NZ)])


def twin(x):
    return lax.ppermute(x, "c", [(0, 1), (1, 0)])


def swap_across(x):
    pairs = [(4 * p + 2 * b + c, 4 * (1 - p) + 2 * c + b) for p in range(2) for b in range(2) for c in range(2)]
    return lax.ppermute(x, ("p", "b", "c"), pairs)


def nothing(x):
    return x[0, 0].astype(f32) * 0.0


def add(*terms):
    total = terms[0].astype(f32)
    for x in terms[1:]:
        total = total + x.astype(f32)
    return total.astype(bf16)


def body(queries, key_rows, value_rows, out_grads, doc_ids, owner_plan):
    n = NZ * NY
    me = lax.axis_index(OWNER)
    p, c = lax.axis_index("p"), lax.axis_index("c")
    rows, width = queries.shape
    pieces = jnp.arange(n, dtype=jnp.int32)
    owners = lax.dynamic_index_in_dim(owner_plan, me, 0, keepdims=False)

    r = jnp.arange(rows, dtype=jnp.int32)
    owner_row = jnp.repeat(owners, PIECE) * PIECE + r % PIECE
    onehot = (r[:, None] == owner_row[None, :]).astype(bf16)
    outgoing = jnp.dot(onehot, swap(queries), preferred_element_type=f32).astype(bf16)
    q = lax.all_to_all(outgoing.reshape(n, PIECE, width), OWNER, 0, 0, tiled=True).reshape(rows, width)

    mine = jnp.concatenate([key_rows, value_rows], axis=1)
    mine = jnp.concatenate([swap(mine), swap_across(mine)], axis=0)
    g = lax.all_to_all(add(out_grads, nothing(mine)), ("x", "c"), split_axis=1, concat_axis=0, tiled=True)
    g = swap(g)
    ups, downs = [mine], [mine]
    for step in range(NZ // 2):
        ups.append(ring(ups[-1], 1))
        if step < NZ // 2 - 1:
            downs.append(ring(downs[-1], -1))
    own = ups + downs[:0:-1]
    twins = [twin(x) for x in own]

    slot_of = jnp.sum(jnp.where(owner_plan == me, pieces[None, :], 0), axis=1)
    place = (
        pieces[:, None] * TOK + slot_of[:, None] * PIECE + jnp.arange(PIECE, dtype=jnp.int32)[None, :]
    ).reshape(GROUPS, 1, 1, rows // GROUPS)
    docs = jnp.arange(DOCS, dtype=jnp.int32)
    doc_first = jnp.sum((doc_ids[:, None] < docs[None, :]).astype(jnp.int32), axis=0)
    start = jnp.max(jnp.where(doc_first <= place[..., None], doc_first, 0), axis=-1)
    lo = jnp.min(start, axis=(1, 2, 3)) // PLANE
    hi = jnp.max(place, axis=(1, 2, 3)) // PLANE + 1
    spread_lanes = lambda x: jnp.broadcast_to(x, (GROUPS, 1, width // HD, rows // GROUPS)).reshape(GROUPS, 1, -1)
    at = jnp.stack([me // NY] + [2 * (p ^ (j & 1)) + (c ^ (j >> 1)) for j in range(NY)])

    o, dq, keep, give = attend(lo, hi, at, spread_lanes(place), spread_lanes(start), q, g, own, twins)

    returned = lax.all_to_all(dq.reshape(n, PIECE, width), OWNER, 0, 0, tiled=True).reshape(rows, width)
    o = swap(o)
    attention = lax.all_to_all(add(o, nothing(returned)), ("x", "c"), split_axis=0, concat_axis=1, tiled=True)
    query_grads = swap(jnp.dot(onehot.T, returned, preferred_element_type=f32).astype(bf16))

    got = [None] * NZ
    for r in (4, 5, 3, 6, 2, 7, 1, 0):
        got[r] = twin(give[r])
    up = ring(add(keep[4], got[4]), 1)
    down = ring(add(keep[5], got[5]), -1)
    for r in (3, 2, 1):
        up = ring(add(keep[r], got[r], up, *([nothing(o)] if r == 2 else [])), 1)
        if r > 1:
            down = ring(add(keep[9 - r], got[9 - r], down), -1)
    total = add(keep[0], got[0], up, down, nothing(query_grads))
    grads = add(swap(total[:TOK]), swap_across(total[TOK:]))

    return attention, query_grads, grads[:, :HD], grads[:, HD:]


def solution(mesh):
    ctx, head = ("z", "p", "b"), ("x", "c")
    fine = Mesh(mesh.devices.reshape(NZ, 2, 2, -1, 2), AXES)
    rows = P(ctx + head, None)
    return jax.shard_map(
        body,
        mesh=fine,
        in_specs=(P(ctx, head),) * 3 + (rows, P(), P()),
        out_specs=(rows,) + (P(ctx, head),) * 3,
        check_vma=False,
    )
```

```python
import jax
import jax.numpy as jnp
from jax import lax
from jax.experimental import pallas as pl
from jax.experimental.pallas import tpu as pltpu
from jax.sharding import Mesh
from jax.sharding import PartitionSpec as P

HD = 128
NZ = 8
NY = 4
TOK = 256
PLANE = NY * TOK
PIECE = 8
DOCLEN = 4096
DOCS = 8
GROUPS = 8
MOST = DOCLEN // PLANE + 1
MASKED = -1e30
LOG2E = 1.4426950408889634
f32 = jnp.float32
bf16 = jnp.bfloat16


def attend_kernel(lo_ref, hi_ref, at_ref, place_ref, start_ref, q_ref, g_ref, *refs):
    own_refs, twin_refs = refs[:NZ], refs[NZ : 2 * NZ]
    refs = refs[2 * NZ :]
    o_ref, dq_ref = refs[:2]
    keep_refs, give_refs = refs[2 : 2 + NZ], refs[2 + NZ : 2 + 2 * NZ]
    kn, vn, dk_acc, dv_acc, s_ref, e_ref = refs[2 + 2 * NZ :]
    rows, width = q_ref.shape
    heads = width // HD
    span = rows // GROUPS
    lanes = span * heads
    scale = HD**-0.5
    half = PLANE // 2
    my_z = at_ref[0]

    for rz in range(NZ):
        z = lax.rem(my_z + NZ - rz, NZ)
        for part, refs_of in ((slice(0, half), own_refs), (slice(half, PLANE), twin_refs)):
            kn[z, part, :] = refs_of[rz][:, :HD]
            vn[z, part, :] = refs_of[rz][:, HD:]

    def gather_heads(ref, at):
        x = ref[at, :]
        return jnp.concatenate([x[:, h * HD : (h + 1) * HD] for h in range(heads)], axis=0)

    def scatter_heads(ref, at, x):
        for h in range(heads):
            ref[at, h * HD : (h + 1) * HD] = x[h * span : (h + 1) * span]

    ones = jnp.ones((8, PLANE), bf16)

    def score(kb, slot, own_plane, qt, place, start, peak):
        s = jnp.dot(kn[kb], qt, preferred_element_type=f32)
        u = lax.broadcasted_iota(jnp.int32, (TOK, lanes), 0)
        for ry in range(NY):
            base = kb * PLANE + at_ref[1 + ry] * TOK
            part = s[ry * TOK : (ry + 1) * TOK]
            seen = u >= start - base
            if own_plane:
                seen = seen & (u <= place - base)
            part = jnp.where(seen, part, MASKED)
            s_ref[slot, ry * TOK : (ry + 1) * TOK, :] = part
            peak = jnp.maximum(peak, jnp.max(part.reshape(TOK // 8, 8, lanes), axis=0))
        return peak

    def weigh(kb, slot, peak, ot, total):
        e = jnp.exp2(s_ref[slot] * (scale * LOG2E) - peak)
        eb = e.astype(bf16)
        e_ref[slot] = eb
        total = total + jnp.dot(ones, eb, preferred_element_type=f32)
        return ot + lax.dot_general(vn[kb], eb, (((0,), (0,)), ((), ())), preferred_element_type=f32), total

    def back(kb, slot, own_plane, gt, delta, qs, gs, dqt):
        dp = jnp.dot(vn[kb], gt, preferred_element_type=f32)
        eb = e_ref[slot]
        ds = (eb.astype(f32) * (dp - delta)).astype(bf16)
        dk = jnp.dot(ds, qs, preferred_element_type=f32)
        dv = jnp.dot(eb, gs, preferred_element_type=f32)
        if own_plane:
            dk_acc[kb] = dk
            dv_acc[kb] = dv
        else:
            dk_acc[kb] += dk
            dv_acc[kb] += dv
        return dqt + lax.dot_general(kn[kb], ds, (((0,), (0,)), ((), ())), preferred_element_type=f32)

    def group(gi, carry):
        at = pl.ds(pl.multiple_of(gi * span, span), span)
        lo = lo_ref[gi]
        place, start = place_ref[gi], start_ref[gi]
        qt = gather_heads(q_ref, at).astype(f32).T
        gt = gather_heads(g_ref, at).astype(f32).T
        qtb, gtb = qt.astype(bf16), gt.astype(bf16)

        peak = score(gi, 0, True, qtb, place, start, jnp.full((8, lanes), MASKED, f32))
        peak = lax.fori_loop(
            lo, gi, lambda kb, x: score(kb, 1 + kb - lo, False, qtb, place, start, x), peak
        )
        peak = jnp.max(peak, axis=0, keepdims=True) * (scale * LOG2E)

        zero = (jnp.zeros((HD, lanes), f32), jnp.zeros((8, lanes), f32))
        ot, total = lax.fori_loop(
            lo, gi, lambda kb, x: weigh(kb, 1 + kb - lo, peak, *x), weigh(gi, 0, peak, *zero)
        )
        inverse = 1.0 / total[:1]
        otb = (ot * inverse).astype(bf16).astype(f32)
        scatter_heads(o_ref, at, otb.T.astype(bf16))
        delta = jnp.sum(otb * gt, axis=0, keepdims=True)
        qs = (qt * inverse).T.astype(bf16)
        gs = (gt * inverse).T.astype(bf16)

        dqt = back(gi, 0, True, gtb, delta, qs, gs, jnp.zeros((HD, lanes), f32))
        dqt = lax.fori_loop(
            lo, gi, lambda kb, x: back(kb, 1 + kb - lo, False, gtb, delta, qs, gs, x), dqt
        )
        scatter_heads(dq_ref, at, (dqt * (inverse * scale)).T.astype(bf16))
        return carry

    lax.fori_loop(0, GROUPS, group, 0)

    for rz in range(NZ):
        z = lax.rem(my_z + rz, NZ)
        for part, refs_of in ((slice(0, half), keep_refs), (slice(half, PLANE), give_refs)):
            refs_of[rz][:, :HD] = (dk_acc[z, part, :] * scale).astype(bf16)
            refs_of[rz][:, HD:] = dv_acc[z, part, :].astype(bf16)


def attend(lo, hi, at, place, start, q, g, own, twin):
    rows, width = q.shape
    lanes = rows // GROUPS * (width // HD)
    vm = pl.BlockSpec(memory_space=pltpu.VMEM)
    sm = pl.BlockSpec(memory_space=pltpu.SMEM)
    outs = (
        [jax.ShapeDtypeStruct((rows, width), bf16)] * 2
        + [jax.ShapeDtypeStruct((PLANE // 2, 2 * HD), bf16)] * (2 * NZ)
    )
    out = pl.pallas_call(
        attend_kernel,
        in_specs=[sm] * 3 + [vm] * (4 + 2 * NZ),
        out_specs=[vm] * len(outs),
        out_shape=outs,
        scratch_shapes=[
            pltpu.VMEM((NZ, PLANE, HD), bf16),
            pltpu.VMEM((NZ, PLANE, HD), bf16),
            pltpu.VMEM((NZ, PLANE, HD), f32),
            pltpu.VMEM((NZ, PLANE, HD), f32),
            pltpu.VMEM((MOST, PLANE, lanes), f32),
            pltpu.VMEM((MOST, PLANE, lanes), bf16),
        ],
        compiler_params=pltpu.CompilerParams(vmem_limit_bytes=52 * 1024 * 1024),
        cost_estimate=pl.CostEstimate(
            flops=12 * 10**9, bytes_accessed=12 * 10**6, transcendentals=4 * 10**6
        ),
        name="attend",
    )(lo, hi, at, place, start, q, g, *own, *twin)
    return out[0], out[1], out[2 : 2 + NZ], out[2 + NZ :]


AXES = ("z", "p", "b", "x", "c")
OWNER = ("z", "p", "c")


def swap(x):
    return lax.ppermute(x, ("b", "c"), [(0, 0), (1, 2), (2, 1), (3, 3)])


def ring(x, step):
    return lax.ppermute(x, "z", [(i, (i + step) % NZ) for i in range(NZ)])


def twin(x):
    return lax.ppermute(x, "c", [(0, 1), (1, 0)])


def swap_across(x):
    pairs = [(4 * p + 2 * b + c, 4 * (1 - p) + 2 * c + b) for p in range(2) for b in range(2) for c in range(2)]
    return lax.ppermute(x, ("p", "b", "c"), pairs)


def nothing(x):
    return x[0, 0].astype(f32) * 0.0


def add(*terms):
    total = terms[0].astype(f32)
    for x in terms[1:]:
        total = total + x.astype(f32)
    return total.astype(bf16)


def body(queries, key_rows, value_rows, out_grads, doc_ids, owner_plan):
    n = NZ * NY
    me = lax.axis_index(OWNER)
    p, c = lax.axis_index("p"), lax.axis_index("c")
    rows, width = queries.shape
    pieces = jnp.arange(n, dtype=jnp.int32)
    owners = lax.dynamic_index_in_dim(owner_plan, me, 0, keepdims=False)

    r = jnp.arange(rows, dtype=jnp.int32)
    owner_row = jnp.repeat(owners, PIECE) * PIECE + r % PIECE
    onehot = (r[:, None] == owner_row[None, :]).astype(bf16)
    outgoing = jnp.dot(onehot, swap(queries), preferred_element_type=f32).astype(bf16)
    q = lax.all_to_all(outgoing.reshape(n, PIECE, width), OWNER, 0, 0, tiled=True).reshape(rows, width)

    mine = jnp.concatenate([key_rows, value_rows], axis=1)
    mine = jnp.concatenate([swap(mine), swap_across(mine)], axis=0)
    g = lax.all_to_all(add(out_grads, nothing(mine)), ("x", "c"), split_axis=1, concat_axis=0, tiled=True)
    g = swap(g)
    ups, downs = [mine], [mine]
    for step in range(NZ // 2):
        ups.append(ring(ups[-1], 1))
        if step < NZ // 2 - 1:
            downs.append(ring(downs[-1], -1))
    own = ups + downs[:0:-1]
    twins = [twin(x) for x in own]

    slot_of = jnp.sum(jnp.where(owner_plan == me, pieces[None, :], 0), axis=1)
    place = (
        pieces[:, None] * TOK + slot_of[:, None] * PIECE + jnp.arange(PIECE, dtype=jnp.int32)[None, :]
    ).reshape(GROUPS, 1, 1, rows // GROUPS)
    docs = jnp.arange(DOCS, dtype=jnp.int32)
    doc_first = jnp.sum((doc_ids[:, None] < docs[None, :]).astype(jnp.int32), axis=0)
    start = jnp.max(jnp.where(doc_first <= place[..., None], doc_first, 0), axis=-1)
    lo = jnp.min(start, axis=(1, 2, 3)) // PLANE
    hi = jnp.max(place, axis=(1, 2, 3)) // PLANE + 1
    spread_lanes = lambda x: jnp.broadcast_to(x, (GROUPS, 1, width // HD, rows // GROUPS)).reshape(GROUPS, 1, -1)
    at = jnp.stack([me // NY] + [2 * (p ^ (j & 1)) + (c ^ (j >> 1)) for j in range(NY)])

    o, dq, keep, give = attend(lo, hi, at, spread_lanes(place), spread_lanes(start), q, g, own, twins)

    returned = lax.all_to_all(dq.reshape(n, PIECE, width), OWNER, 0, 0, tiled=True).reshape(rows, width)
    o = swap(o)
    attention = lax.all_to_all(add(o, nothing(returned)), ("x", "c"), split_axis=0, concat_axis=1, tiled=True)
    query_grads = swap(jnp.dot(onehot.T, returned, preferred_element_type=f32).astype(bf16))

    got = [None] * NZ
    for r in (4, 5, 3, 6, 2, 7, 1, 0):
        got[r] = twin(give[r])
    up = ring(add(keep[4], got[4]), 1)
    down = ring(add(keep[5], got[5]), -1)
    for r in (3, 2, 1):
        up = ring(add(keep[r], got[r], up, *([nothing(o), nothing(returned)] if r == 1 else [])), 1)
        if r > 1:
            down = ring(add(keep[9 - r], got[9 - r], down), -1)
    total = add(keep[0], got[0], up, down)
    near, far = swap(total[:TOK]), swap_across(total[TOK:])
    key_grads, value_grads = (add(near[:, cols], far[:, cols]) for cols in (slice(0, HD), slice(HD, 2 * HD)))

    return attention, query_grads, key_grads, value_grads


def solution(mesh):
    ctx, head = ("z", "p", "b"), ("x", "c")
    fine = Mesh(mesh.devices.reshape(NZ, 2, 2, -1, 2), AXES)
    rows = P(ctx + head, None)
    return jax.shard_map(
        body,
        mesh=fine,
        in_specs=(P(ctx, head),) * 3 + (rows, P(), P()),
        out_specs=(rows,) + (P(ctx, head),) * 3,
        check_vma=False,
    )
```
